32 devices in a mesh: dp: 4 (over x, core), space: 8 (over z, y).
Axes of the slice: x: 2, y: 2, z: 4, core: 2. Of those that a mesh axis runs over, the one named last changes fastest.
Arguments:
- features: bfloat16 [4, 32, 256, 512], P('dp', None, 'space'), may hold values from -6 to 6
- cotangent: bfloat16 [4, 32, 256, 512], P('dp', None, 'space'), may hold values from -6 to 6
- conv_kernel: float32 [7, 7, 512], replicated, may hold values from -0.875 to 0.875
- conv_bias: float32 [512], replicated, may hold values from -3 to 3
- norm_gain: float32 [512], replicated, may hold values from 0.5 to 1.5
- norm_bias: float32 [512], replicated, may hold values from -3 to 3
- weight_in: bfloat16 [512, 2048], P(('dp', 'space')), may hold values from -0.25 to 0.25
- bias_in: float32 [2048], replicated, may hold values from -3 to 3
- weight_out: bfloat16 [2048, 512], P(('dp', 'space')), may hold values from -0.125 to 0.125
- bias_out: float32 [512], replicated, may hold values from -3 to 3
- layer_scale: float32 [512], replicated, may hold values from 0.3 to 1.5
Outputs:
- block_out: bfloat16 [4, 32, 256, 512], P('dp', None, 'space')
- grad_features: bfloat16 [4, 32, 256, 512], P('dp', None, 'space')
- grad_kernel: float32 [7, 7, 512], replicated
- grad_convbias: float32 [512], replicated
- grad_gain: float32 [512], replicated
- grad_normbias: float32 [512], replicated
- grad_inproj: float32 [512, 2048], P(('dp', 'space'))
- grad_inbias: float32 [2048], replicated
- grad_outproj: float32 [2048, 512], P(('dp', 'space'))
- grad_outbias: float32 [512], replicated
- grad_scale: float32 [512], replicated
The draws below stay inside these ranges and needn't reach their ends.
All inputs are finite; a program needn't handle non-finite values.
Results may differ from the reference program's by a relative error of at most 0.009.
Values may be sent and summed in bfloat16 or wider, within the bound.
A program may use at most 576 MiB of HBM per device.

```python
import math
import jax
import jax.numpy as jnp
from jax import lax

C = 512
HID = 2048
KS = 7
ROWS = 32
COLS = 256
SLABS = 4


def block_levels(own_key, dims, split, least, high):
    def one(axis_at, parts):
        draws = jax.random.uniform(jax.random.fold_in(jax.random.fold_in(own_key, 6), axis_at), (parts,), jnp.float32, least / len(split), high / len(split))
        return jnp.repeat(jnp.exp(draws), dims[axis_at] // parts).reshape((-1,) + (1,) * (len(dims) - axis_at - 1))

    factor_of = one(*split[0])
    for cut in split[1:]:
        factor_of = factor_of * one(*cut)
    return factor_of


def bell_draw(own_key, shape, scale, most, cuts=(), kind=jnp.bfloat16):
    level = block_levels(own_key, shape, cuts, -0.22, 0.18) if cuts else 1.0
    result = jax.random.normal(own_key, shape, jnp.float32) * scale * level
    return jnp.minimum(jnp.maximum(result, -most), most).astype(kind)


def setup_inputs(seed: int = 0) -> dict:
    key_of = jax.random.split(jax.random.key(seed), 12)
    return {
        "features": bell_draw(key_of[0], (SLABS, ROWS, COLS, C), 1.0, 6.0, ((0, 4), (2, 8))),
        "cotangent": bell_draw(key_of[1], (SLABS, ROWS, COLS, C), 1.0, 6.0, ((0, 4), (2, 8))),
        "conv_kernel": bell_draw(key_of[2], (KS, KS, C), (KS * KS) ** -0.5, 0.875, (), jnp.float32),
        "conv_bias": bell_draw(key_of[3], (C,), 0.5, 3.0, (), jnp.float32),
        "norm_gain": jnp.clip(jax.random.uniform(key_of[4], (C,), jnp.float32, 0.5, 1.5), 0.5, 1.5),
        "norm_bias": bell_draw(key_of[5], (C,), 0.5, 3.0, (), jnp.float32),
        "weight_in": bell_draw(key_of[6], (C, HID), C ** -0.5, 0.25, ((0, 32),)),
        "bias_in": bell_draw(key_of[7], (HID,), 0.5, 3.0, (), jnp.float32),
        "weight_out": bell_draw(key_of[8], (HID, C), HID ** -0.5, 0.125, ((0, 32),)),
        "bias_out": bell_draw(key_of[9], (C,), 0.5, 3.0, (), jnp.float32),
        "layer_scale": jnp.clip(jnp.exp(jax.random.uniform(key_of[10], (C,), jnp.float32, math.log(0.3), math.log(1.5))), 0.3, 1.5),
    }


NORM_EPS = 1e-06

def gelu_exact(inputs):
    return jax.nn.gelu(inputs, approximate=False)

def conv_forward(padded, kernel, offset, row_count, col_count):
    summed = jnp.zeros((row_count, col_count, padded.shape[2]), jnp.float32)
    for tap_row in range(KS):
        for tap_col in range(KS):
            window = padded[tap_row:tap_row + row_count, tap_col:tap_col + col_count].astype(jnp.float32)
            summed = summed + kernel[tap_row, tap_col] * window
    return (summed + offset).astype(jnp.bfloat16)

def conv_backward(grad_padded, kernel, row_count, col_count):
    summed = jnp.zeros((row_count, col_count, grad_padded.shape[2]), jnp.float32)
    for tap_row in range(KS):
        for tap_col in range(KS):
            row_start = KS - 1 - tap_row
            col_start = KS - 1 - tap_col
            window = grad_padded[row_start:row_start + row_count, col_start:col_start + col_count].astype(jnp.float32)
            summed = summed + kernel[tap_row, tap_col] * window
    return summed

def kernel_gradient(grad_conv, padded, row_count, col_count):
    grad_wide = grad_conv.astype(jnp.float32)
    taps = []
    for tap_row in range(KS):
        tap_line = []
        for tap_col in range(KS):
            window = padded[tap_row:tap_row + row_count, tap_col:tap_col + col_count].astype(jnp.float32)
            tap_line.append(lax.optimization_barrier(jnp.sum(grad_wide * window, axis=(0, 1))))
        taps.append(jnp.stack(tap_line))
    return jnp.stack(taps)

def norm_mlp(conv_out, source, upstream, norm_gain, norm_bias, weight_in, bias_in, weight_out, bias_out, layer_scale):
    widened = conv_out.astype(jnp.float32)
    center = lax.optimization_barrier(jnp.mean(widened, axis=-1, keepdims=True))
    shifted = widened - center
    inv_std = lax.rsqrt(lax.optimization_barrier(jnp.mean(shifted * shifted, axis=-1, keepdims=True)) + NORM_EPS)
    normed = shifted * inv_std
    activated = (normed * norm_gain + norm_bias).astype(jnp.bfloat16)
    pre_act = jnp.dot(activated, weight_in, preferred_element_type=jnp.float32) + bias_in
    hidden_wide, gelu_back = jax.vjp(gelu_exact, pre_act)
    hidden = hidden_wide.astype(jnp.bfloat16)
    branch = jnp.dot(hidden, weight_out, preferred_element_type=jnp.float32) + bias_out
    block_out = (source.astype(jnp.float32) + layer_scale * branch).astype(jnp.bfloat16)
    upstream_wide = upstream.astype(jnp.float32)
    d_branch = layer_scale * upstream_wide
    d_branch_b = d_branch.astype(jnp.bfloat16)
    grad_scale = lax.optimization_barrier(jnp.sum(upstream_wide * branch, axis=0))
    grad_outbias = lax.optimization_barrier(jnp.sum(d_branch, axis=0))
    grad_outproj = lax.dot_general(hidden, d_branch_b, (((0,), (0,)), ((), ())), preferred_element_type=jnp.float32)
    d_hidden = lax.dot_general(d_branch_b, weight_out, (((1,), (1,)), ((), ())), preferred_element_type=jnp.float32)
    d_pre = gelu_back(d_hidden)[0]
    d_pre_b = d_pre.astype(jnp.bfloat16)
    grad_inbias = lax.optimization_barrier(jnp.sum(d_pre, axis=0))
    grad_inproj = lax.dot_general(activated, d_pre_b, (((0,), (0,)), ((), ())), preferred_element_type=jnp.float32)
    d_act = lax.dot_general(d_pre_b, weight_in, (((1,), (1,)), ((), ())), preferred_element_type=jnp.float32)
    grad_gain = lax.optimization_barrier(jnp.sum(d_act * normed, axis=0))
    grad_normbias = lax.optimization_barrier(jnp.sum(d_act, axis=0))
    scaled = d_act * norm_gain
    grad_conv = inv_std * (scaled - lax.optimization_barrier(jnp.mean(scaled, axis=-1, keepdims=True)) - normed * lax.optimization_barrier(jnp.mean(scaled * normed, axis=-1, keepdims=True)))
    return (block_out, grad_conv.astype(jnp.bfloat16), (grad_gain, grad_normbias, grad_inproj, grad_inbias, grad_outproj, grad_outbias, grad_scale))

def reference(features, cotangent, conv_kernel, conv_bias, norm_gain, norm_bias, weight_in, bias_in, weight_out, bias_out, layer_scale):
    reach = KS // 2
    block_size = math.gcd(ROWS * COLS, 2048)
    totals = (jnp.zeros((C,), jnp.float32), jnp.zeros((C,), jnp.float32), jnp.zeros((C, HID), jnp.float32), jnp.zeros((HID,), jnp.float32), jnp.zeros((HID, C), jnp.float32), jnp.zeros((C,), jnp.float32), jnp.zeros((C,), jnp.float32))
    kernel_total = jnp.zeros((KS, KS, C), jnp.float32)
    convbias_total = jnp.zeros((C,), jnp.float32)
    outputs = []
    grads = []

    def scan_step(carried, inputs):
        conv_block, source_block, upstream_block = inputs
        out_block, grad_block, partials = norm_mlp(conv_block, source_block, upstream_block, norm_gain, norm_bias, weight_in, bias_in, weight_out, bias_out, layer_scale)
        return (tuple((left + right for left, right in zip(carried, partials))), (out_block, grad_block))
    for slab_idx in range(SLABS):
        source = features[slab_idx]
        upstream = cotangent[slab_idx]
        padded = jnp.pad(source, ((reach, reach), (reach, reach), (0, 0)))
        conv_out = conv_forward(padded, conv_kernel, conv_bias, ROWS, COLS)
        scan_inputs = (conv_out.reshape(-1, block_size, C), source.reshape(-1, block_size, C), upstream.reshape(-1, block_size, C))
        totals, (out_blocks, grad_blocks) = lax.scan(scan_step, totals, scan_inputs)
        grad_conv = grad_blocks.reshape(ROWS, COLS, C)
        grad_padded = jnp.pad(grad_conv, ((reach, reach), (reach, reach), (0, 0)))
        conv_back = conv_backward(grad_padded, conv_kernel, ROWS, COLS)
        grads.append((upstream.astype(jnp.float32) + conv_back).astype(jnp.bfloat16))
        outputs.append(out_blocks.reshape(ROWS, COLS, C))
        kernel_total = kernel_total + kernel_gradient(grad_conv, padded, ROWS, COLS)
        convbias_total = convbias_total + lax.optimization_barrier(jnp.sum(grad_conv.astype(jnp.float32), axis=(0, 1)))
    grad_gain, grad_normbias, grad_inproj, grad_inbias, grad_outproj, grad_outbias, grad_scale = totals
    return (jnp.stack(outputs), jnp.stack(grads), kernel_total, convbias_total, grad_gain, grad_normbias, grad_inproj, grad_inbias, grad_outproj, grad_outbias, grad_scale)
```

```python
import jax
import jax.numpy as jnp
from jax import lax
from jax.sharding import PartitionSpec as P

KS = 7


NORM_EPS = 1e-06


def padded_2(x, sides, width):
    for axis, dim in sides:
        peers, length = (lax.axis_size(axis), x.shape[dim])
        up = [(i, (i + 1) % peers) for i in range(peers - 1)]
        down = [(j, i) for i, j in up]
        last = lax.slice_in_dim(x, length - width, length, axis=dim)
        initial = lax.slice_in_dim(x, 0, width, axis=dim)
        before = lax.ppermute(last, axis, up)
        after = lax.ppermute(initial, axis, down)
        x = jnp.concatenate([before, x, after], axis=dim)
    return x


def index_bits():
    listed = []
    for axis in ("dp", "space"):
        stride = 1
        while stride < lax.axis_size(axis):
            listed.append((axis, stride))
            stride *= 2
    return listed


def row_order(key):
    return (key[0] != "dp", -key[1])


def swapped(x, key):
    axis, stride = key
    return lax.ppermute(x, axis, [(i, i ^ stride) for i in range(lax.axis_size(axis))])


def own_bit(key):
    return (lax.axis_index(key[0]) // key[1]) % 2


def gather_rows(x):
    tail = x.shape[1]
    present = []
    for key in index_bits()[::-1]:
        other = swapped(x, key)
        present = sorted(present + [key], key=row_order)
        at = present.index(key)
        high = own_bit(key) == 1
        x = jnp.stack([jnp.where(high, other, x), jnp.where(high, x, other)], axis=at)
    return x.reshape(-1, tail)


def scatter_sum_rows(x):
    keys = index_bits()
    present = sorted(keys, key=row_order)
    x = x.reshape((2,) * len(keys) + (-1, x.shape[1]))
    for key in keys:
        at = present.index(key)
        bit = own_bit(key)
        kept = lax.dynamic_index_in_dim(x, bit, at, keepdims=False)
        sent = lax.dynamic_index_in_dim(x, 1 - bit, at, keepdims=False).astype(jnp.bfloat16)
        x = kept + swapped(sent, key).astype(jnp.float32)
        present.remove(key)
    return x


def sum_everywhere(parts):
    flat = jnp.concatenate([part.reshape(-1, parts[0].shape[-1]) for part in parts])
    for key in index_bits():
        flat = flat + swapped(flat, key)
    outs, at = [], 0
    for part in parts:
        rows = part.size // flat.shape[1]
        outs.append(flat[at : at + rows].reshape(part.shape))
        at += rows
    return outs


def gelu_exact(inputs):
    return jax.nn.gelu(inputs, approximate=False)


def conv_forward(padded, kernel, offset, row_count, col_count):
    summed = jnp.zeros((row_count, col_count, padded.shape[2]), jnp.float32)
    for tap_row in range(KS):
        for tap_col in range(KS):
            window = padded[tap_row : tap_row + row_count, tap_col : tap_col + col_count].astype(
                jnp.float32
            )
            summed = summed + kernel[tap_row, tap_col] * window
    return (summed + offset).astype(jnp.bfloat16)


def conv_backward(grad_padded, kernel, row_count, col_count):
    summed = jnp.zeros((row_count, col_count, grad_padded.shape[2]), jnp.float32)
    for tap_row in range(KS):
        for tap_col in range(KS):
            row_start = KS - 1 - tap_row
            col_start = KS - 1 - tap_col
            window = grad_padded[
                row_start : row_start + row_count, col_start : col_start + col_count
            ].astype(jnp.float32)
            summed = summed + kernel[tap_row, tap_col] * window
    return summed


def kernel_gradient(grad_conv, padded, row_count, col_count):
    grad_wide = grad_conv.astype(jnp.float32)
    taps = []
    for tap_row in range(KS):
        tap_line = []
        for tap_col in range(KS):
            window = padded[tap_row : tap_row + row_count, tap_col : tap_col + col_count].astype(
                jnp.float32
            )
            tap_line.append(jnp.sum(grad_wide * window, axis=(0, 1)))
        taps.append(jnp.stack(tap_line))
    return jnp.stack(taps)


def norm_mlp(
    conv_out,
    source,
    upstream,
    norm_gain,
    norm_bias,
    weight_in,
    bias_in,
    weight_out,
    bias_out,
    layer_scale,
):
    widened = conv_out.astype(jnp.float32)
    center = jnp.mean(widened, axis=-1, keepdims=True)
    shifted = widened - center
    inv_std = lax.rsqrt(jnp.mean(shifted * shifted, axis=-1, keepdims=True) + NORM_EPS)
    normed = shifted * inv_std
    activated = (normed * norm_gain + norm_bias).astype(jnp.bfloat16)
    pre_act = jnp.dot(activated, weight_in, preferred_element_type=jnp.float32) + bias_in
    hidden_wide, gelu_back = jax.vjp(gelu_exact, pre_act)
    hidden = hidden_wide.astype(jnp.bfloat16)
    branch = jnp.dot(hidden, weight_out, preferred_element_type=jnp.float32) + bias_out
    block_out = (source.astype(jnp.float32) + layer_scale * branch).astype(jnp.bfloat16)
    upstream_wide = upstream.astype(jnp.float32)
    d_branch = layer_scale * upstream_wide
    d_branch_b = d_branch.astype(jnp.bfloat16)
    grad_scale = jnp.sum(upstream_wide * branch, axis=0)
    grad_outbias = jnp.sum(d_branch, axis=0)
    grad_outproj = lax.dot_general(
        hidden, d_branch_b, (((0,), (0,)), ((), ())), preferred_element_type=jnp.float32
    )
    d_hidden = lax.dot_general(
        d_branch_b, weight_out, (((1,), (1,)), ((), ())), preferred_element_type=jnp.float32
    )
    d_pre = gelu_back(d_hidden)[0]
    d_pre_b = d_pre.astype(jnp.bfloat16)
    grad_inbias = jnp.sum(d_pre, axis=0)
    grad_inproj = lax.dot_general(
        activated, d_pre_b, (((0,), (0,)), ((), ())), preferred_element_type=jnp.float32
    )
    d_act = lax.dot_general(
        d_pre_b, weight_in, (((1,), (1,)), ((), ())), preferred_element_type=jnp.float32
    )
    grad_gain = jnp.sum(d_act * normed, axis=0)
    grad_normbias = jnp.sum(d_act, axis=0)
    scaled = d_act * norm_gain
    grad_conv = inv_std * (
        scaled
        - jnp.mean(scaled, axis=-1, keepdims=True)
        - normed * jnp.mean(scaled * normed, axis=-1, keepdims=True)
    )
    return (
        block_out,
        grad_conv.astype(jnp.bfloat16),
        (
            grad_gain,
            grad_normbias,
            grad_inproj,
            grad_inbias,
            grad_outproj,
            grad_outbias,
            grad_scale,
        ),
    )


def local(
    features,
    cotangent,
    conv_kernel,
    conv_bias,
    norm_gain,
    norm_bias,
    weight_in,
    bias_in,
    weight_out,
    bias_out,
    layer_scale,
):
    reach = KS // 2
    source = features[0]
    upstream = cotangent[0]
    row_count, col_count, channels = source.shape
    full_in, full_out = (
        gather_rows(weight_in),
        gather_rows(weight_out),
    )
    rimmed = padded_2(source, (("space", 1),), reach)
    padded = jnp.pad(rimmed, ((reach, reach), (0, 0), (0, 0)))
    conv_out = conv_forward(padded, conv_kernel, conv_bias, row_count, col_count)
    block_out, grad_conv, partials = norm_mlp(
        conv_out.reshape(-1, channels),
        source.reshape(-1, channels),
        upstream.reshape(-1, channels),
        norm_gain,
        norm_bias,
        full_in,
        bias_in,
        full_out,
        bias_out,
        layer_scale,
    )
    grad_conv = grad_conv.reshape(row_count, col_count, channels)
    grad_rimmed = padded_2(grad_conv, (("space", 1),), reach)
    grad_padded = jnp.pad(grad_rimmed, ((reach, reach), (0, 0), (0, 0)))
    conv_back = conv_backward(grad_padded, conv_kernel, row_count, col_count)
    grad_kern = kernel_gradient(grad_conv, padded, row_count, col_count)
    grad_cbias = jnp.sum(grad_conv.astype(jnp.float32), axis=(0, 1))
    grad_feat = (upstream.astype(jnp.float32) + conv_back).astype(jnp.bfloat16)
    grad_gain, grad_normbias, grad_inproj, grad_inbias, grad_outproj, grad_outbias, grad_scale = (
        partials
    )
    early = sum_everywhere((grad_gain, grad_normbias, grad_inbias, grad_outbias, grad_scale))
    late = sum_everywhere((grad_kern, grad_cbias))
    reduced = late + early
    owned_in, owned_out = (scatter_sum_rows(grad_inproj), scatter_sum_rows(grad_outproj))
    return (
        block_out.reshape(1, row_count, col_count, channels),
        grad_feat[None],
        reduced[0],
        reduced[1],
        reduced[2],
        reduced[3],
        owned_in,
        reduced[4],
        owned_out,
        reduced[5],
        reduced[6],
    )


def solution(mesh):
    return jax.shard_map(
        local,
        mesh=mesh,
        in_specs=(
            P("dp", None, "space", None),
            P("dp", None, "space", None),
            P(),
            P(),
            P(),
            P(),
            P(("dp", "space"), None),
            P(),
            P(("dp", "space"), None),
            P(),
            P(),
        ),
        out_specs=(
            P("dp", None, "space", None),
            P("dp", None, "space", None),
            P(),
            P(),
            P(),
            P(),
            P(("dp", "space"), None),
            P(),
            P(("dp", "space"), None),
            P(),
            P(),
        ),
        check_vma=False,
    )
```

```python
import jax
import jax.numpy as jnp
from jax import lax
from jax.experimental import pallas as pl
from jax.experimental.pallas import tpu as pltpu
from jax.sharding import PartitionSpec as P

KS = 7


NORM_EPS = 1e-06


def padded_2(x, sides, width):
    for axis, dim in sides:
        peers, length = (lax.axis_size(axis), x.shape[dim])
        up = [(i, (i + 1) % peers) for i in range(peers - 1)]
        down = [(j, i) for i, j in up]
        last = lax.slice_in_dim(x, length - width, length, axis=dim)
        initial = lax.slice_in_dim(x, 0, width, axis=dim)
        before = lax.ppermute(last, axis, up)
        after = lax.ppermute(initial, axis, down)
        x = jnp.concatenate([before, x, after], axis=dim)
    return x


def index_bits(other_order=False):
    listed = []
    for axis in ("dp", "space"):
        stride = 1
        while stride < lax.axis_size(axis):
            listed.append((axis, stride))
            stride *= 2
    if other_order:
        listed[1], listed[2] = listed[2], listed[1]
    return listed


def row_order(key):
    return (key[0] != "dp", -key[1])


def swapped(x, key):
    axis, stride = key
    return lax.ppermute(x, axis, [(i, i ^ stride) for i in range(lax.axis_size(axis))])


def own_bit(key):
    return (lax.axis_index(key[0]) // key[1]) % 2


def gather_rows(x, other_order=False):
    tail = x.shape[1]
    present = []
    for key in index_bits(other_order)[::-1]:
        other = swapped(x, key)
        present = sorted(present + [key], key=row_order)
        at = present.index(key)
        high = own_bit(key) == 1
        x = jnp.stack([jnp.where(high, other, x), jnp.where(high, x, other)], axis=at)
    return x.reshape(-1, tail)


def scatter_sum_rows(x, other_order=False):
    keys = index_bits(other_order)
    present = sorted(keys, key=row_order)
    x = x.reshape((2,) * len(keys) + (-1, x.shape[1]))
    for key in keys:
        at = present.index(key)
        bit = own_bit(key)
        kept = lax.dynamic_index_in_dim(x, bit, at, keepdims=False)
        sent = lax.dynamic_index_in_dim(x, 1 - bit, at, keepdims=False).astype(jnp.bfloat16)
        x = kept.astype(jnp.float32) + swapped(sent, key).astype(jnp.float32)
        present.remove(key)
    return x


def sum_everywhere(parts):
    flat = jnp.concatenate([part.reshape(-1, parts[0].shape[-1]) for part in parts])
    for key in index_bits():
        flat = flat + swapped(flat, key)
    outs, at = [], 0
    for part in parts:
        rows = part.size // flat.shape[1]
        outs.append(flat[at : at + rows].reshape(part.shape))
        at += rows
    return outs


def conv_forward(padded, kernel, offset, row_count, col_count):
    summed = jnp.zeros((row_count, col_count, padded.shape[2]), jnp.float32)
    for tap_row in range(KS):
        for tap_col in range(KS):
            window = padded[tap_row : tap_row + row_count, tap_col : tap_col + col_count].astype(
                jnp.float32
            )
            summed = summed + kernel[tap_row, tap_col] * window
    return (summed + offset).astype(jnp.bfloat16)


def conv_backward(grad_padded, kernel, row_count, col_count):
    summed = jnp.zeros((row_count, col_count, grad_padded.shape[2]), jnp.float32)
    for tap_row in range(KS):
        for tap_col in range(KS):
            row_start = KS - 1 - tap_row
            col_start = KS - 1 - tap_col
            window = grad_padded[
                row_start : row_start + row_count, col_start : col_start + col_count
            ].astype(jnp.float32)
            summed = summed + kernel[tap_row, tap_col] * window
    return summed


def kernel_gradient(grad_conv, padded, row_count, col_count):
    grad_wide = grad_conv.astype(jnp.float32)
    taps = []
    for tap_row in range(KS):
        tap_line = []
        for tap_col in range(KS):
            window = padded[tap_row : tap_row + row_count, tap_col : tap_col + col_count].astype(
                jnp.float32
            )
            tap_line.append(jnp.sum(grad_wide * window, axis=(0, 1)))
        taps.append(jnp.stack(tap_line))
    return jnp.stack(taps)


def dot(a, b, over_a, over_b):
    return lax.dot_general(
        a, b, (((over_a,), (over_b,)), ((), ())), preferred_element_type=jnp.float32
    )


def norm_mlp_kernel(
    conv_ref,
    source_ref,
    upstream_ref,
    gain_ref,
    bias_ref,
    win_ref,
    bin_ref,
    wout_ref,
    bout_ref,
    scale_ref,
    block_ref,
    gconv_ref,
    ggain_ref,
    gnbias_ref,
    gin_ref,
    ginbias_ref,
    gout_ref,
    goutbias_ref,
    gscale_ref,
    gcbias_ref,
    normed,
    inv_std,
    act,
    dbranch,
    branch,
    dact,
):
    step = pl.program_id(0)

    @pl.when(step == 0)
    def _():
        wide = conv_ref[...].astype(jnp.float32)
        shifted = wide - jnp.mean(wide, axis=-1, keepdims=True)
        inv = lax.rsqrt(jnp.mean(shifted * shifted, axis=-1, keepdims=True) + NORM_EPS)
        inv_std[...] = inv
        unit = shifted * inv
        normed[...] = unit
        act[...] = (unit * gain_ref[...] + bias_ref[...]).astype(jnp.bfloat16)
        d_branch = scale_ref[...] * upstream_ref[...].astype(jnp.float32)
        goutbias_ref[...] = jnp.sum(d_branch, axis=0, keepdims=True)
        dbranch[...] = d_branch.astype(jnp.bfloat16)
        branch[...] = jnp.zeros_like(branch)
        dact[...] = jnp.zeros_like(dact)

    pre = dot(act[...], win_ref[...], 1, 0) + bin_ref[...]
    d_hidden = dot(dbranch[...], wout_ref[...], 1, 1)
    cdf = 0.5 + 0.5 * lax.erf(pre * 0.7071067811865476)
    slope = cdf + pre * (jnp.exp(pre * pre * -0.5) * 0.3989422804014327)
    hidden = (pre * cdf).astype(jnp.bfloat16)
    d_pre = d_hidden * slope
    ginbias_ref[...] = jnp.sum(d_pre, axis=0, keepdims=True)
    d_pre_b = d_pre.astype(jnp.bfloat16)
    branch[...] += dot(hidden, wout_ref[...], 1, 0)
    gout_ref[...] = dot(hidden, dbranch[...], 0, 0).astype(jnp.bfloat16)
    dact[...] += dot(d_pre_b, win_ref[...], 1, 1)
    gin_ref[...] = dot(act[...], d_pre_b, 0, 0).astype(jnp.bfloat16)

    @pl.when(step == pl.num_programs(0) - 1)
    def _():
        full = branch[...] + bout_ref[...]
        block_ref[...] = (source_ref[...].astype(jnp.float32) + scale_ref[...] * full).astype(
            jnp.bfloat16
        )
        gscale_ref[...] = jnp.sum(upstream_ref[...].astype(jnp.float32) * full, 0, keepdims=True)
        d_act = dact[...]
        unit = normed[...]
        ggain_ref[...] = jnp.sum(d_act * unit, axis=0, keepdims=True)
        gnbias_ref[...] = jnp.sum(d_act, axis=0, keepdims=True)
        scaled = d_act * gain_ref[...]
        grad = inv_std[...] * (
            scaled
            - jnp.mean(scaled, axis=-1, keepdims=True)
            - unit * jnp.mean(scaled * unit, axis=-1, keepdims=True)
        )
        grad_b = grad.astype(jnp.bfloat16)
        gconv_ref[...] = grad_b
        gcbias_ref[...] = jnp.sum(grad_b.astype(jnp.float32), axis=0, keepdims=True)


def norm_mlp(
    conv_out,
    source,
    upstream,
    norm_gain,
    norm_bias,
    weight_in,
    bias_in,
    weight_out,
    bias_out,
    layer_scale,
):
    pixels, channels = conv_out.shape
    units = weight_in.shape[1]
    tile = 256
    whole = pl.BlockSpec((pixels, channels), lambda i: (0, 0))
    row = pl.BlockSpec((1, channels), lambda i: (0, 0))
    columns = pl.BlockSpec((channels, tile), lambda i: (0, i))
    rows = pl.BlockSpec((tile, channels), lambda i: (i, 0))
    unit_row = pl.BlockSpec((1, tile), lambda i: (0, i))
    f32, bf16 = jnp.float32, jnp.bfloat16
    shape = jax.ShapeDtypeStruct
    vector = shape((1, channels), f32)
    flops = 12 * pixels * channels * units
    return pl.pallas_call(
        norm_mlp_kernel,
        grid=(units // tile,),
        in_specs=[whole, whole, whole, row, row, columns, unit_row, rows, row, row],
        out_specs=[whole, whole, row, row, columns, unit_row, rows, row, row, row],
        out_shape=[
            shape((pixels, channels), bf16),
            shape((pixels, channels), bf16),
            vector,
            vector,
            shape((channels, units), bf16),
            shape((1, units), f32),
            shape((units, channels), bf16),
            vector,
            vector,
            vector,
        ],
        scratch_shapes=[
            pltpu.VMEM((pixels, channels), f32),
            pltpu.VMEM((pixels, 1), f32),
            pltpu.VMEM((pixels, channels), bf16),
            pltpu.VMEM((pixels, channels), bf16),
            pltpu.VMEM((pixels, channels), f32),
            pltpu.VMEM((pixels, channels), f32),
        ],
        compiler_params=pltpu.CompilerParams(vmem_limit_bytes=48 * 1024 * 1024),
        cost_estimate=pl.CostEstimate(
            flops=flops, bytes_accessed=16 * 1024 * 1024, transcendentals=pixels * units
        ),
    )(
        conv_out,
        source,
        upstream,
        norm_gain[None],
        norm_bias[None],
        weight_in,
        bias_in[None],
        weight_out,
        bias_out[None],
        layer_scale[None],
    )


def local(
    features,
    cotangent,
    conv_kernel,
    conv_bias,
    norm_gain,
    norm_bias,
    weight_in,
    bias_in,
    weight_out,
    bias_out,
    layer_scale,
):
    reach = KS // 2
    source = features[0]
    upstream = cotangent[0]
    row_count, col_count, channels = source.shape
    full_in, full_out = (
        gather_rows(weight_in),
        gather_rows(weight_out, True),
    )
    rimmed = padded_2(source, (("space", 1),), reach)
    padded = jnp.pad(rimmed, ((reach, reach), (0, 0), (0, 0)))
    conv_out = conv_forward(padded, conv_kernel, conv_bias, row_count, col_count)
    block_out, grad_conv, *partials = norm_mlp(
        conv_out.reshape(-1, channels),
        source.reshape(-1, channels),
        upstream.reshape(-1, channels),
        norm_gain,
        norm_bias,
        full_in,
        bias_in,
        full_out,
        bias_out,
        layer_scale,
    )
    grad_conv = grad_conv.reshape(row_count, col_count, channels)
    grad_rimmed = padded_2(grad_conv, (("space", 1),), reach)
    grad_padded = jnp.pad(grad_rimmed, ((reach, reach), (0, 0), (0, 0)))
    conv_back = conv_backward(grad_padded, conv_kernel, row_count, col_count)
    grad_kern = kernel_gradient(grad_conv, padded, row_count, col_count)
    grad_feat = (upstream.astype(jnp.float32) + conv_back).astype(jnp.bfloat16)
    (
        grad_gain,
        grad_normbias,
        grad_inproj,
        grad_inbias,
        grad_outproj,
        grad_outbias,
        grad_scale,
        grad_cbias,
    ) = partials
    reduced = sum_everywhere(
        (grad_kern, grad_cbias, grad_gain, grad_normbias, grad_inbias, grad_outbias, grad_scale)
    )
    owned_in, owned_out = (scatter_sum_rows(grad_inproj), scatter_sum_rows(grad_outproj, True))
    return (
        block_out.reshape(1, row_count, col_count, channels),
        grad_feat[None],
        reduced[0],
        reduced[1].reshape(-1),
        reduced[2].reshape(-1),
        reduced[3].reshape(-1),
        owned_in,
        reduced[4].reshape(-1),
        owned_out,
        reduced[5].reshape(-1),
        reduced[6].reshape(-1),
    )


def solution(mesh):
    return jax.shard_map(
        local,
        mesh=mesh,
        in_specs=(
            P("dp", None, "space", None),
            P("dp", None, "space", None),
            P(),
            P(),
            P(),
            P(),
            P(("dp", "space"), None),
            P(),
            P(("dp", "space"), None),
            P(),
            P(),
        ),
        out_specs=(
            P("dp", None, "space", None),
            P("dp", None, "space", None),
            P(),
            P(),
            P(),
            P(),
            P(("dp", "space"), None),
            P(),
            P(("dp", "space"), None),
            P(),
            P(),
        ),
        check_vma=False,
    )
```

```python
import jax
import jax.numpy as jnp
from jax import lax
from jax.experimental import pallas as pl
from jax.experimental.pallas import tpu as pltpu
from jax.sharding import PartitionSpec as P

KS = 7


NORM_EPS = 1e-06


def padded_2(x, sides, width):
    for axis, dim in sides:
        peers, length = (lax.axis_size(axis), x.shape[dim])
        up = [(i, (i + 1) % peers) for i in range(peers - 1)]
        down = [(j, i) for i, j in up]
        last = lax.slice_in_dim(x, length - width, length, axis=dim)
        initial = lax.slice_in_dim(x, 0, width, axis=dim)
        before = lax.ppermute(last, axis, up)
        after = lax.ppermute(initial, axis, down)
        x = jnp.concatenate([before, x, after], axis=dim)
    return x


def index_bits(other_order=False):
    listed = []
    for axis in ("dp", "space"):
        stride = 1
        while stride < lax.axis_size(axis):
            listed.append((axis, stride))
            stride *= 2
    if other_order:
        listed[1], listed[2] = listed[2], listed[1]
    return listed


def row_order(key):
    return (key[0] != "dp", -key[1])


def swapped(x, key):
    axis, stride = key
    return lax.ppermute(x, axis, [(i, i ^ stride) for i in range(lax.axis_size(axis))])


def own_bit(key):
    return (lax.axis_index(key[0]) // key[1]) % 2


def gather_step(x, other, present, key):
    present.append(key)
    present.sort(key=row_order)
    high = own_bit(key) == 1
    return jnp.stack(
        [jnp.where(high, other, x), jnp.where(high, x, other)], axis=present.index(key)
    )


def halves(x, present, key):
    at = present.index(key)
    bit = own_bit(key)
    present.remove(key)
    kept = lax.dynamic_index_in_dim(x, bit, at, keepdims=False).astype(jnp.float32)
    sent = lax.dynamic_index_in_dim(x, 1 - bit, at, keepdims=False).astype(jnp.bfloat16)
    return kept, sent


def tied(*values):
    return lax.optimization_barrier(values)


def gather_beside(weight_in, weight_out, source, works):
    in_keys, out_keys = index_bits()[::-1], index_bits(True)[::-1]
    in_present, out_present, done = [], [], []
    first, second = weight_in, weight_out
    for k, (in_key, out_key) in enumerate(zip(in_keys, out_keys)):
        place = k - (len(in_keys) - len(works))
        if place >= 0:
            first, second, source = tied(first, second, source)
        first_other, second_other = swapped(first, in_key), swapped(second, out_key)
        if place >= 0:
            result = works[place](source)
            first_other, second_other, result = tied(first_other, second_other, result)
            done.append(result)
        first = gather_step(first, first_other, in_present, in_key)
        second = gather_step(second, second_other, out_present, out_key)
    return first.reshape(-1, weight_in.shape[1]), second.reshape(-1, weight_out.shape[1]), done


def conv_forward(padded, kernel, offset, row_count, col_count):
    summed = jnp.zeros((row_count, col_count, padded.shape[2]), jnp.float32)
    for tap_row in range(KS):
        for tap_col in range(KS):
            window = padded[tap_row : tap_row + row_count, tap_col : tap_col + col_count].astype(
                jnp.float32
            )
            summed = summed + kernel[tap_row, tap_col] * window
    return (summed + offset).astype(jnp.bfloat16)


def conv_backward(grad_padded, kernel, row_count, col_count):
    summed = jnp.zeros((row_count, col_count, grad_padded.shape[2]), jnp.float32)
    for tap_row in range(KS):
        for tap_col in range(KS):
            row_start = KS - 1 - tap_row
            col_start = KS - 1 - tap_col
            window = grad_padded[
                row_start : row_start + row_count, col_start : col_start + col_count
            ].astype(jnp.float32)
            summed = summed + kernel[tap_row, tap_col] * window
    return summed


def kernel_gradient(grad_conv, padded, row_count, col_count, tap_rows):
    grad_wide = grad_conv.astype(jnp.float32)
    taps = []
    for tap_row in tap_rows:
        for tap_col in range(KS):
            window = padded[tap_row : tap_row + row_count, tap_col : tap_col + col_count].astype(
                jnp.float32
            )
            taps.append(jnp.sum(grad_wide * window, axis=(0, 1)))
    return taps


def dot(a, b, over_a, over_b):
    return lax.dot_general(
        a, b, (((over_a,), (over_b,)), ((), ())), preferred_element_type=jnp.float32
    )


def norm_mlp_kernel(
    conv_ref,
    source_ref,
    upstream_ref,
    gain_ref,
    bias_ref,
    win_ref,
    bin_ref,
    wout_ref,
    bout_ref,
    scale_ref,
    block_ref,
    gconv_ref,
    ggain_ref,
    gnbias_ref,
    gin_ref,
    ginbias_ref,
    gout_ref,
    goutbias_ref,
    gscale_ref,
    gcbias_ref,
    normed,
    inv_std,
    act,
    dbranch,
    branch,
    dact,
):
    step = pl.program_id(0)

    @pl.when(step == 0)
    def _():
        wide = conv_ref[...].astype(jnp.float32)
        shifted = wide - jnp.mean(wide, axis=-1, keepdims=True)
        inv = lax.rsqrt(jnp.mean(shifted * shifted, axis=-1, keepdims=True) + NORM_EPS)
        inv_std[...] = inv
        unit = shifted * inv
        normed[...] = unit
        act[...] = (unit * gain_ref[...] + bias_ref[...]).astype(jnp.bfloat16)
        d_branch = scale_ref[...] * upstream_ref[...].astype(jnp.float32)
        goutbias_ref[...] = jnp.sum(d_branch, axis=0, keepdims=True)
        dbranch[...] = d_branch.astype(jnp.bfloat16)
        branch[...] = jnp.zeros_like(branch)
        dact[...] = jnp.zeros_like(dact)

    pre = dot(act[...], win_ref[...], 1, 0) + bin_ref[...]
    d_hidden = dot(dbranch[...], wout_ref[...], 1, 1)
    cdf = 0.5 + 0.5 * lax.erf(pre * 0.7071067811865476)
    slope = cdf + pre * (jnp.exp(pre * pre * -0.5) * 0.3989422804014327)
    hidden = (pre * cdf).astype(jnp.bfloat16)
    d_pre = d_hidden * slope
    ginbias_ref[...] = jnp.sum(d_pre, axis=0, keepdims=True)
    d_pre_b = d_pre.astype(jnp.bfloat16)
    branch[...] += dot(hidden, wout_ref[...], 1, 0)
    gout_ref[...] = dot(hidden, dbranch[...], 0, 0).astype(jnp.bfloat16)
    dact[...] += dot(d_pre_b, win_ref[...], 1, 1)
    gin_ref[...] = dot(act[...], d_pre_b, 0, 0).astype(jnp.bfloat16)

    @pl.when(step == pl.num_programs(0) - 1)
    def _():
        full = branch[...] + bout_ref[...]
        block_ref[...] = (source_ref[...].astype(jnp.float32) + scale_ref[...] * full).astype(
            jnp.bfloat16
        )
        gscale_ref[...] = jnp.sum(upstream_ref[...].astype(jnp.float32) * full, 0, keepdims=True)
        d_act = dact[...]
        unit = normed[...]
        ggain_ref[...] = jnp.sum(d_act * unit, axis=0, keepdims=True)
        gnbias_ref[...] = jnp.sum(d_act, axis=0, keepdims=True)
        scaled = d_act * gain_ref[...]
        grad = inv_std[...] * (
            scaled
            - jnp.mean(scaled, axis=-1, keepdims=True)
            - unit * jnp.mean(scaled * unit, axis=-1, keepdims=True)
        )
        grad_b = grad.astype(jnp.bfloat16)
        gconv_ref[...] = grad_b
        gcbias_ref[...] = jnp.sum(grad_b.astype(jnp.float32), axis=0, keepdims=True)


def norm_mlp(
    conv_out,
    source,
    upstream,
    norm_gain,
    norm_bias,
    weight_in,
    bias_in,
    weight_out,
    bias_out,
    layer_scale,
):
    pixels, channels = conv_out.shape
    units = weight_in.shape[1]
    tile = 256
    whole = pl.BlockSpec((pixels, channels), lambda i: (0, 0))
    row = pl.BlockSpec((1, channels), lambda i: (0, 0))
    columns = pl.BlockSpec((channels, tile), lambda i: (0, i))
    rows = pl.BlockSpec((tile, channels), lambda i: (i, 0))
    unit_row = pl.BlockSpec((1, tile), lambda i: (0, i))
    f32, bf16 = jnp.float32, jnp.bfloat16
    shape = jax.ShapeDtypeStruct
    vector = shape((1, channels), f32)
    flops = 12 * pixels * channels * units
    return pl.pallas_call(
        norm_mlp_kernel,
        grid=(units // tile,),
        in_specs=[whole, whole, whole, row, row, columns, unit_row, rows, row, row],
        out_specs=[whole, whole, row, row, columns, unit_row, rows, row, row, row],
        out_shape=[
            shape((pixels, channels), bf16),
            shape((pixels, channels), bf16),
            vector,
            vector,
            shape((channels, units), bf16),
            shape((1, units), f32),
            shape((units, channels), bf16),
            vector,
            vector,
            vector,
        ],
        scratch_shapes=[
            pltpu.VMEM((pixels, channels), f32),
            pltpu.VMEM((pixels, 1), f32),
            pltpu.VMEM((pixels, channels), bf16),
            pltpu.VMEM((pixels, channels), bf16),
            pltpu.VMEM((pixels, channels), f32),
            pltpu.VMEM((pixels, channels), f32),
        ],
        compiler_params=pltpu.CompilerParams(vmem_limit_bytes=48 * 1024 * 1024),
        cost_estimate=pl.CostEstimate(
            flops=flops, bytes_accessed=16 * 1024 * 1024, transcendentals=pixels * units
        ),
    )(
        conv_out,
        source,
        upstream,
        norm_gain[None],
        norm_bias[None],
        weight_in,
        bias_in[None],
        weight_out,
        bias_out[None],
        layer_scale[None],
    )


def local(
    features,
    cotangent,
    conv_kernel,
    conv_bias,
    norm_gain,
    norm_bias,
    weight_in,
    bias_in,
    weight_out,
    bias_out,
    layer_scale,
):
    reach = KS // 2
    source = features[0]
    upstream = cotangent[0]
    row_count, col_count, channels = source.shape
    rimmed = padded_2(source, (("space", 1),), reach)
    padded = jnp.pad(rimmed, ((reach, reach), (0, 0), (0, 0)))
    half = row_count // 2

    def conv_rows(start):
        return lambda x: conv_forward(
            x[start : start + half + KS - 1], conv_kernel, conv_bias, half, col_count
        )

    full_in, full_out, conv_halves = gather_beside(
        weight_in, weight_out, padded, (conv_rows(0), conv_rows(half))
    )
    conv_out = jnp.concatenate(conv_halves)
    block_out, grad_conv, *partials = norm_mlp(
        conv_out.reshape(-1, channels),
        source.reshape(-1, channels),
        upstream.reshape(-1, channels),
        norm_gain,
        norm_bias,
        full_in,
        bias_in,
        full_out,
        bias_out,
        layer_scale,
    )
    grad_conv = grad_conv.reshape(row_count, col_count, channels)
    grad_rimmed = padded_2(grad_conv, (("space", 1),), reach)
    grad_padded = jnp.pad(grad_rimmed, ((reach, reach), (0, 0), (0, 0)))
    (
        grad_gain,
        grad_normbias,
        grad_inproj,
        grad_inbias,
        grad_outproj,
        grad_outbias,
        grad_scale,
        grad_cbias,
    ) = partials
    in_keys, out_keys = index_bits(), index_bits(True)
    in_present, out_present = sorted(in_keys, key=row_order), sorted(out_keys, key=row_order)
    first = grad_inproj.reshape((2,) * len(in_keys) + (-1, grad_inproj.shape[1]))
    second = grad_outproj.reshape((2,) * len(out_keys) + (-1, channels))
    small_keys = list(in_keys)
    small = None
    taps, back = [], []
    for k, (in_key, out_key) in enumerate(zip(in_keys, out_keys)):
        first_kept, first_sent = halves(first, in_present, in_key)
        second_kept, second_sent = halves(second, out_present, out_key)
        if k < 2:
            first_sent, second_sent, g, p = tied(first_sent, second_sent, grad_conv, padded)
            first_got, second_got = swapped(first_sent, in_key), swapped(second_sent, out_key)
            rows = range(2) if k == 0 else range(2, KS)
            result = kernel_gradient(g, p, row_count, col_count, rows)
            first_got, second_got, result = tied(first_got, second_got, result)
            taps += result
            if k == 1:
                parts = (
                    grad_cbias,
                    grad_gain,
                    grad_normbias,
                    grad_inbias,
                    grad_outbias,
                    grad_scale,
                )
                small = jnp.concatenate(
                    [jnp.stack(taps)] + [part.reshape(-1, channels) for part in parts]
                )
        else:
            first_sent, second_sent, small, p = tied(first_sent, second_sent, small, grad_padded)
            first_got, second_got = swapped(first_sent, in_key), swapped(second_sent, out_key)
            small_got = swapped(small, small_keys.pop(0))
            result = ()
            if k < 4:
                start = (k - 2) * half
                window = p[start : start + half + KS - 1]
                wide = conv_backward(window, conv_kernel, half, col_count)
                wide = wide + upstream[start : start + half].astype(jnp.float32)
                result = wide.astype(jnp.bfloat16)
            first_got, second_got, small_got, result = tied(
                first_got, second_got, small_got, result
            )
            small = small + small_got
            if k < 4:
                back.append(result)
        first = first_kept + first_got.astype(jnp.float32)
        second = second_kept + second_got.astype(jnp.float32)
    for key in small_keys:
        small = small + swapped(small, key)
    owned_in, owned_out = first, second
    grad_feat = jnp.concatenate(back)
    reduced, at = [small[: KS * KS].reshape(KS, KS, channels)], KS * KS
    for part in parts:
        rows = part.size // channels
        reduced.append(small[at : at + rows])
        at += rows
    return (
        block_out.reshape(1, row_count, col_count, channels),
        grad_feat[None],
        reduced[0],
        reduced[1].reshape(-1),
        reduced[2].reshape(-1),
        reduced[3].reshape(-1),
        owned_in,
        reduced[4].reshape(-1),
        owned_out,
        reduced[5].reshape(-1),
        reduced[6].reshape(-1),
    )


def solution(mesh):
    return jax.shard_map(
        local,
        mesh=mesh,
        in_specs=(
            P("dp", None, "space", None),
            P("dp", None, "space", None),
            P(),
            P(),
            P(),
            P(),
            P(("dp", "space"), None),
            P(),
            P(("dp", "space"), None),
            P(),
            P(),
        ),
        out_specs=(
            P("dp", None, "space", None),
            P("dp", None, "space", None),
            P(),
            P(),
            P(),
            P(),
            P(("dp", "space"), None),
            P(),
            P(("dp", "space"), None),
            P(),
            P(),
        ),
        check_vma=False,
    )
```

```python
import jax
import jax.numpy as jnp
from jax import lax
from jax.experimental import pallas as pl
from jax.experimental.pallas import tpu as pltpu
from jax.sharding import PartitionSpec as P

KS = 7


NORM_EPS = 1e-06


def padded_2(x, sides, width):
    for axis, dim in sides:
        peers, length = (lax.axis_size(axis), x.shape[dim])
        up = [(i, (i + 1) % peers) for i in range(peers - 1)]
        down = [(j, i) for i, j in up]
        last = lax.slice_in_dim(x, length - width, length, axis=dim)
        initial = lax.slice_in_dim(x, 0, width, axis=dim)
        before = lax.ppermute(last, axis, up)
        after = lax.ppermute(initial, axis, down)
        x = jnp.concatenate([before, x, after], axis=dim)
    return x


def index_bits(other_order=False):
    listed = []
    for axis in ("dp", "space"):
        stride = 1
        while stride < lax.axis_size(axis):
            listed.append((axis, stride))
            stride *= 2
    if other_order:
        listed[1], listed[2] = listed[2], listed[1]
    return listed


def row_order(key):
    return (key[0] != "dp", -key[1])


def swapped(x, key):
    axis, stride = key
    return lax.ppermute(x, axis, [(i, i ^ stride) for i in range(lax.axis_size(axis))])


def own_bit(key):
    return (lax.axis_index(key[0]) // key[1]) % 2


def gather_step(x, other, present, key):
    present.append(key)
    present.sort(key=row_order)
    high = own_bit(key) == 1
    return jnp.stack(
        [jnp.where(high, other, x), jnp.where(high, x, other)], axis=present.index(key)
    )


def halves(x, present, key):
    at = present.index(key)
    bit = own_bit(key)
    present.remove(key)
    kept = lax.dynamic_index_in_dim(x, bit, at, keepdims=False).astype(jnp.float32)
    sent = lax.dynamic_index_in_dim(x, 1 - bit, at, keepdims=False).astype(jnp.bfloat16)
    return kept, sent


def tied(*values):
    return lax.optimization_barrier(values)


def gather_beside(weight_in, weight_out, source, works):
    in_keys, out_keys = index_bits()[::-1], index_bits(True)[::-1]
    in_present, out_present, done = [], [], []
    first, second = weight_in, weight_out
    for k, (in_key, out_key) in enumerate(zip(in_keys, out_keys)):
        place = k - (len(in_keys) - len(works))
        if place >= 0:
            first, second, source = tied(first, second, source)
        first_other, second_other = swapped(first, in_key), swapped(second, out_key)
        if place >= 0:
            result = works[place](source)
            first_other, second_other, result = tied(first_other, second_other, result)
            done.append(result)
        first = gather_step(first, first_other, in_present, in_key)
        second = gather_step(second, second_other, out_present, out_key)
    return first.reshape(-1, weight_in.shape[1]), second.reshape(-1, weight_out.shape[1]), done


def conv_forward(padded, kernel, offset, row_count, col_count):
    summed = jnp.zeros((row_count, col_count, padded.shape[2]), jnp.float32)
    for tap_row in range(KS):
        for tap_col in range(KS):
            window = padded[tap_row : tap_row + row_count, tap_col : tap_col + col_count].astype(
                jnp.float32
            )
            summed = summed + kernel[tap_row, tap_col] * window
    return (summed + offset).astype(jnp.bfloat16)


def conv_backward(grad_padded, kernel, row_count, col_count):
    summed = jnp.zeros((row_count, col_count, grad_padded.shape[2]), jnp.float32)
    for tap_row in range(KS):
        for tap_col in range(KS):
            row_start = KS - 1 - tap_row
            col_start = KS - 1 - tap_col
            window = grad_padded[
                row_start : row_start + row_count, col_start : col_start + col_count
            ].astype(jnp.float32)
            summed = summed + kernel[tap_row, tap_col] * window
    return summed


def kernel_gradient(grad_conv, padded, row_count, col_count, tap_rows):
    grad_wide = grad_conv.astype(jnp.float32)
    taps = []
    for tap_row in tap_rows:
        for tap_col in range(KS):
            window = padded[tap_row : tap_row + row_count, tap_col : tap_col + col_count].astype(
                jnp.float32
            )
            taps.append(jnp.sum(grad_wide * window, axis=(0, 1)))
    return taps


def dot(a, b, over_a, over_b):
    return lax.dot_general(
        a, b, (((over_a,), (over_b,)), ((), ())), preferred_element_type=jnp.float32
    )


def norm_mlp_kernel(
    conv_ref,
    source_ref,
    upstream_ref,
    gain_ref,
    bias_ref,
    win_ref,
    bin_ref,
    wout_ref,
    bout_ref,
    scale_ref,
    block_ref,
    gconv_ref,
    ggain_ref,
    gnbias_ref,
    gin_ref,
    ginbias_ref,
    gout_ref,
    goutbias_ref,
    gscale_ref,
    gcbias_ref,
    normed,
    inv_std,
    act,
    dbranch,
    branch,
    dact,
):
    step = pl.program_id(0)

    @pl.when(step == 0)
    def _():
        wide = conv_ref[...].astype(jnp.float32)
        shifted = wide - jnp.mean(wide, axis=-1, keepdims=True)
        inv = lax.rsqrt(jnp.mean(shifted * shifted, axis=-1, keepdims=True) + NORM_EPS)
        inv_std[...] = inv
        unit = shifted * inv
        normed[...] = unit
        act[...] = (unit * gain_ref[...] + bias_ref[...]).astype(jnp.bfloat16)
        d_branch = scale_ref[...] * upstream_ref[...].astype(jnp.float32)
        goutbias_ref[...] = jnp.sum(d_branch, axis=0, keepdims=True)
        dbranch[...] = d_branch.astype(jnp.bfloat16)
        branch[...] = jnp.zeros_like(branch)
        dact[...] = jnp.zeros_like(dact)

    pre = dot(act[...], win_ref[...], 1, 0) + bin_ref[...]
    d_hidden = dot(dbranch[...], wout_ref[...], 1, 1)
    cdf = 0.5 + 0.5 * lax.erf(pre * 0.7071067811865476)
    slope = cdf + pre * (jnp.exp(pre * pre * -0.5) * 0.3989422804014327)
    hidden = (pre * cdf).astype(jnp.bfloat16)
    d_pre = d_hidden * slope
    ginbias_ref[...] = jnp.sum(d_pre, axis=0, keepdims=True)
    d_pre_b = d_pre.astype(jnp.bfloat16)
    branch[...] += dot(hidden, wout_ref[...], 1, 0)
    gout_ref[...] = dot(hidden, dbranch[...], 0, 0).astype(jnp.bfloat16)
    dact[...] += dot(d_pre_b, win_ref[...], 1, 1)
    gin_ref[...] = dot(act[...], d_pre_b, 0, 0).astype(jnp.bfloat16)

    @pl.when(step == pl.num_programs(0) - 1)
    def _():
        full = branch[...] + bout_ref[...]
        block_ref[...] = (source_ref[...].astype(jnp.float32) + scale_ref[...] * full).astype(
            jnp.bfloat16
        )
        gscale_ref[...] = jnp.sum(upstream_ref[...].astype(jnp.float32) * full, 0, keepdims=True)
        d_act = dact[...]
        unit = normed[...]
        ggain_ref[...] = jnp.sum(d_act * unit, axis=0, keepdims=True)
        gnbias_ref[...] = jnp.sum(d_act, axis=0, keepdims=True)
        scaled = d_act * gain_ref[...]
        grad = inv_std[...] * (
            scaled
            - jnp.mean(scaled, axis=-1, keepdims=True)
            - unit * jnp.mean(scaled * unit, axis=-1, keepdims=True)
        )
        grad_b = grad.astype(jnp.bfloat16)
        gconv_ref[...] = grad_b
        gcbias_ref[...] = jnp.sum(grad_b.astype(jnp.float32), axis=0, keepdims=True)


def norm_mlp(
    conv_out,
    source,
    upstream,
    norm_gain,
    norm_bias,
    weight_in,
    bias_in,
    weight_out,
    bias_out,
    layer_scale,
):
    pixels, channels = conv_out.shape
    units = weight_in.shape[1]
    tile = 256
    whole = pl.BlockSpec((pixels, channels), lambda i: (0, 0))
    row = pl.BlockSpec((1, channels), lambda i: (0, 0))
    columns = pl.BlockSpec((channels, tile), lambda i: (0, i))
    rows = pl.BlockSpec((tile, channels), lambda i: (i, 0))
    unit_row = pl.BlockSpec((1, tile), lambda i: (0, i))
    f32, bf16 = jnp.float32, jnp.bfloat16
    shape = jax.ShapeDtypeStruct
    vector = shape((1, channels), f32)
    flops = 12 * pixels * channels * units
    return pl.pallas_call(
        norm_mlp_kernel,
        grid=(units // tile,),
        in_specs=[whole, whole, whole, row, row, columns, unit_row, rows, row, row],
        out_specs=[whole, whole, row, row, columns, unit_row, rows, row, row, row],
        out_shape=[
            shape((pixels, channels), bf16),
            shape((pixels, channels), bf16),
            vector,
            vector,
            shape((channels, units), bf16),
            shape((1, units), f32),
            shape((units, channels), bf16),
            vector,
            vector,
            vector,
        ],
        scratch_shapes=[
            pltpu.VMEM((pixels, channels), f32),
            pltpu.VMEM((pixels, 1), f32),
            pltpu.VMEM((pixels, channels), bf16),
            pltpu.VMEM((pixels, channels), bf16),
            pltpu.VMEM((pixels, channels), f32),
            pltpu.VMEM((pixels, channels), f32),
        ],
        compiler_params=pltpu.CompilerParams(vmem_limit_bytes=48 * 1024 * 1024),
        cost_estimate=pl.CostEstimate(
            flops=flops, bytes_accessed=16 * 1024 * 1024, transcendentals=pixels * units
        ),
    )(
        conv_out,
        source,
        upstream,
        norm_gain[None],
        norm_bias[None],
        weight_in,
        bias_in[None],
        weight_out,
        bias_out[None],
        layer_scale[None],
    )


def local(
    features,
    cotangent,
    conv_kernel,
    conv_bias,
    norm_gain,
    norm_bias,
    weight_in,
    bias_in,
    weight_out,
    bias_out,
    layer_scale,
):
    reach = KS // 2
    source = features[0]
    upstream = cotangent[0]
    row_count, col_count, channels = source.shape
    rimmed = padded_2(source, (("space", 1),), reach)
    padded = jnp.pad(rimmed, ((reach, reach), (0, 0), (0, 0)))
    half = row_count // 2

    def conv_rows(start):
        return lambda x: conv_forward(
            x[start : start + half + KS - 1], conv_kernel, conv_bias, half, col_count
        )

    full_in, full_out, conv_halves = gather_beside(
        weight_in, weight_out, padded, (conv_rows(0), conv_rows(half))
    )
    conv_out = jnp.concatenate(conv_halves)
    block_out, grad_conv, *partials = norm_mlp(
        conv_out.reshape(-1, channels),
        source.reshape(-1, channels),
        upstream.reshape(-1, channels),
        norm_gain,
        norm_bias,
        full_in,
        bias_in,
        full_out,
        bias_out,
        layer_scale,
    )
    grad_conv = grad_conv.reshape(row_count, col_count, channels)
    grad_rimmed = padded_2(grad_conv, (("space", 1),), reach)
    grad_padded = jnp.pad(grad_rimmed, ((reach, reach), (0, 0), (0, 0)))
    (
        grad_gain,
        grad_normbias,
        grad_inproj,
        grad_inbias,
        grad_outproj,
        grad_outbias,
        grad_scale,
        grad_cbias,
    ) = partials
    in_keys, out_keys = index_bits(), index_bits(True)
    in_present, out_present = sorted(in_keys, key=row_order), sorted(out_keys, key=row_order)
    first = grad_inproj.reshape((2,) * len(in_keys) + (-1, grad_inproj.shape[1]))
    second = grad_outproj.reshape((2,) * len(out_keys) + (-1, channels))
    small_keys = list(in_keys)
    small = None
    taps, back = [], []
    for k, (in_key, out_key) in enumerate(zip(in_keys, out_keys)):
        first_kept, first_sent = halves(first, in_present, in_key)
        second_kept, second_sent = halves(second, out_present, out_key)
        if k < 2:
            first_sent, second_sent, g, p = tied(first_sent, second_sent, grad_conv, padded)
            first_got, second_got = swapped(first_sent, in_key), swapped(second_sent, out_key)
            rows = range(2) if k == 0 else range(2, KS)
            result = kernel_gradient(g, p, row_count, col_count, rows)
            first_got, second_got, result = tied(first_got, second_got, result)
            taps += result
            if k == 1:
                parts = (
                    grad_cbias,
                    grad_gain,
                    grad_normbias,
                    grad_inbias,
                    grad_outbias,
                    grad_scale,
                )
                small = jnp.concatenate(
                    [jnp.stack(taps)] + [part.reshape(-1, channels) for part in parts]
                )
        else:
            first_sent, second_sent, small, p = tied(first_sent, second_sent, small, grad_padded)
            first_got, second_got = swapped(first_sent, in_key), swapped(second_sent, out_key)
            group = [small_keys.pop(0)]
            if k < 4 and small_keys and small_keys[0][0] == group[0][0]:
                axis, stride = small_keys.pop(0)
                group += [(axis, stride), (axis, stride + group[0][1])]
            small_got = tuple(swapped(small, key) for key in group)
            result = ()
            if k < 4:
                start = (k - 2) * half
                window = p[start : start + half + KS - 1]
                wide = conv_backward(window, conv_kernel, half, col_count)
                wide = wide + upstream[start : start + half].astype(jnp.float32)
                result = wide.astype(jnp.bfloat16)
            first_got, second_got, small_got, result = tied(
                first_got, second_got, small_got, result
            )
            small = small + small_got[0]
            if len(group) == 3:
                small = small + (small_got[1] + small_got[2])
            if k < 4:
                back.append(result)
        first = first_kept + first_got.astype(jnp.float32)
        second = second_kept + second_got.astype(jnp.float32)
    for key in small_keys:
        small = small + swapped(small, key)
    owned_in, owned_out = first, second
    grad_feat = jnp.concatenate(back)
    reduced, at = [small[: KS * KS].reshape(KS, KS, channels)], KS * KS
    for part in parts:
        rows = part.size // channels
        reduced.append(small[at : at + rows])
        at += rows
    return (
        block_out.reshape(1, row_count, col_count, channels),
        grad_feat[None],
        reduced[0],
        reduced[1].reshape(-1),
        reduced[2].reshape(-1),
        reduced[3].reshape(-1),
        owned_in,
        reduced[4].reshape(-1),
        owned_out,
        reduced[5].reshape(-1),
        reduced[6].reshape(-1),
    )


def solution(mesh):
    return jax.shard_map(
        local,
        mesh=mesh,
        in_specs=(
            P("dp", None, "space", None),
            P("dp", None, "space", None),
            P(),
            P(),
            P(),
            P(),
            P(("dp", "space"), None),
            P(),
            P(("dp", "space"), None),
            P(),
            P(),
        ),
        out_specs=(
            P("dp", None, "space", None),
            P("dp", None, "space", None),
            P(),
            P(),
            P(),
            P(),
            P(("dp", "space"), None),
            P(),
            P(("dp", "space"), None),
            P(),
            P(),
        ),
        check_vma=False,
    )
```
